128 devices in a mesh: row: 8 (over y_hi, x), col: 16 (over y_lo, z, core).
Axes of the slice: x: 4, y: 4 (y_hi: 2, y_lo: 2; y = y_hi * 2 + y_lo), z: 4, core: 2. Of those that a mesh axis runs over, the one named last changes fastest.
Arguments:
- layer_input: bfloat16 [32768, 3072], P('col', 'row'), may hold values from -6 to 6
- conv_grad: bfloat16 [32768, 13312], P('col', 'row'), may hold values from -0.03125 to 0.03125
- conv_kernel: float32 [4, 13312], P(None, 'row'), may hold values from -3 to 3
- segment_ids: int32 [32768], P('col'), may hold values from 0 to 257, never falling along the last dimension, each value on 1 to 4096 neighbouring positions
- left_basis: float32 [3072, 192], P('col'), may hold values from -0.4375 to 0.4375
- right_basis: float32 [13312, 416], P('row'), may hold values from -0.3125 to 0.3125
- left_stat: float32 [3072, 192], P('col', 'row'), may hold values from -2 to 2
- right_stat: float32 [13312, 416], P('row', 'col'), may hold values from -2 to 2
- first_moment: float32 [3072, 13312], P('col', 'row'), may hold values from -0.6 to 0.6
- second_moment: float32 [3072, 13312], P('col', 'row'), may hold values from 0.005 to 0.05
Outputs:
- new_left_stat: float32 [3072, 192], P('col', 'row')
- new_right_stat: float32 [13312, 416], P('row', 'col')
- new_first: float32 [3072, 13312], P('col', 'row')
- new_second: float32 [3072, 13312], P('col', 'row')
- direction: float32 [3072, 13312], P('col', 'row')
The draws below stay inside these ranges and needn't reach their ends.
Inputs may be any that keep to these rules, and one draw needn't show every extreme that they name: `segment_ids`: document numbers never fall along the tokens; each document holds 1 to 4096 tokens.
All inputs are finite; a program needn't handle non-finite values.
Results may differ from the reference program's by a relative error of at most 0.0023.
Values may be sent and summed in bfloat16 or wider, within the bound.
A program may use at most 320 MiB of HBM per device.

```python
import math
import jax
import jax.numpy as jnp
import numpy as np
from jax import lax

MODEL_WIDTH = 3072
OUTPUT_CHANNELS = 13312
ZW = 6144
XW = 6656
KW = 4
BL = 192
RIGHT_BLOCK_SIZE = 416
TOKENS = 32768
DOCS = 258
DOC_MAX = 4096


def with_spikes(entries, own_key, source, target, parts, factor):
    def block_of(dim):
        return (jnp.arange(entries.shape[dim]) // (entries.shape[dim] // parts)).reshape((-1,) + (1,) * (entries.ndim - 1 - dim))

    one_side = jax.random.permutation(own_key, parts)[block_of(target)]
    second = (block_of(target) + parts // 2) % parts
    return jnp.where((block_of(source) == one_side) | (block_of(source) == second), factor * entries, entries)


def shard_levels(rng, dims, shards, smallest, high):
    gain, own = 1.0, jax.random.fold_in(rng, 6)
    for position, blocks in shards:
        heights = jnp.exp(jax.random.uniform(jax.random.fold_in(own, position), (blocks,), jnp.float32, smallest / len(shards), high / len(shards)))
        gain = gain * jnp.repeat(heights, dims[position] // blocks).reshape([-1 if axis == position else 1 for axis in range(len(dims))])
    return gain


def profile(count, total, reach, slope):
    portions = [(1 << 20) // math.isqrt(standing ** slope) + 1 for standing in range(2, count + 1)]
    rest, counts = total - reach - (count - 1), [1] * (count - 1)
    while rest > 0:
        candidates = [i for i in range(count - 1) if counts[i] < reach]
        mass, left = sum([portions[i] for i in candidates]), rest
        for i in candidates:
            addition = min(reach - counts[i], max(1, left * portions[i] // mass), rest)
            counts[i] = counts[i] + addition
            rest = rest - addition
    return np.array([reach] + counts)


def ragged(own_key, amount, total, limit, skew):
    if amount == 2:
        one = jax.random.randint(own_key, (), max(1, total - limit), min(limit, total - 1) + 1)
        return jnp.stack([one, total - one])
    sizes = jnp.asarray(profile(amount, total, limit, skew), jnp.int32)
    pairs = (amount - 1) // 2
    source_of, sink = sizes[1:1 + 2 * pairs:2], sizes[2:2 + 2 * pairs:2]
    room = jnp.minimum(source_of - 1, limit - sink)
    passed = jax.random.randint(jax.random.fold_in(own_key, 1), (pairs,), 0, 1 << 20) % (room + 1)
    sizes = sizes.at[1:1 + 2 * pairs:2].set(source_of - passed).at[2:2 + 2 * pairs:2].set(sink + passed)
    return sizes[jax.random.permutation(jax.random.fold_in(own_key, 2), amount)]


def scatter_about(own_key, shape, spread, reach, cuts=(), held_as=jnp.bfloat16):
    entries = spread * jax.random.normal(own_key, shape, jnp.float32)
    if cuts:
        entries = entries * shard_levels(own_key, shape, cuts, -0.22, 0.18)
    return jnp.clip(entries, -reach, reach).astype(held_as)


def noise_with(key, dims, scale, reach, cuts, heavy, kind=jnp.bfloat16):
    drawn = scale * jax.random.normal(key, dims, jnp.float32)
    if cuts:
        drawn = drawn * shard_levels(key, dims, cuts, -0.22, 0.18)
    return jnp.clip(with_spikes(drawn, jax.random.fold_in(key, 3), *heavy), -reach, reach).astype(kind)


def setup_inputs(seed: int = 0) -> dict:
    seeds = jax.random.split(jax.random.key(seed), 11)
    return {
        "layer_input": noise_with(seeds[0], (TOKENS, MODEL_WIDTH), 1.0, 6.0, ((0, 16), (1, 8)), (0, 1, 16, 2.0)),
        "conv_grad": scatter_about(seeds[1], (TOKENS, OUTPUT_CHANNELS), TOKENS ** -0.5, 0.03125, ((0, 16), (1, 8))),
        "conv_kernel": scatter_about(seeds[2], (KW, OUTPUT_CHANNELS), 0.5, 3.0, ((1, 8),), jnp.float32),
        "segment_ids": jnp.searchsorted(jnp.cumsum(ragged(seeds[3], DOCS, TOKENS, DOC_MAX, 1)), jnp.arange(TOKENS), side="right").astype(jnp.int32),
        "left_basis": scatter_about(seeds[4], (MODEL_WIDTH, BL), BL ** -0.5, 0.4375, ((0, 16),), jnp.float32),
        "right_basis": scatter_about(seeds[5], (OUTPUT_CHANNELS, RIGHT_BLOCK_SIZE), RIGHT_BLOCK_SIZE ** -0.5, 0.3125, ((0, 8),), jnp.float32),
        "left_stat": scatter_about(seeds[6], (MODEL_WIDTH, BL), 0.3, 2.0, ((0, 16), (1, 8)), jnp.float32),
        "right_stat": scatter_about(seeds[7], (OUTPUT_CHANNELS, RIGHT_BLOCK_SIZE), 0.3, 2.0, ((0, 8), (1, 16)), jnp.float32),
        "first_moment": scatter_about(seeds[8], (MODEL_WIDTH, OUTPUT_CHANNELS), 0.1, 0.6, ((0, 16), (1, 8)), jnp.float32),
        "second_moment": jnp.clip(jnp.exp(math.log(0.05) - 2.3025851 * jax.random.uniform(seeds[9], (MODEL_WIDTH, OUTPUT_CHANNELS), jnp.float32) ** shard_levels(seeds[9], (MODEL_WIDTH, OUTPUT_CHANNELS), ((0, 16), (1, 8)), -0.2, 0.2)), 0.005, 0.05),
    }


def reference(layer_input, conv_grad, conv_kernel, segment_ids, left_basis, right_basis, left_stat, right_stat, first_moment, second_moment):
    upper_limit = lax.Precision.HIGHEST
    pad_ids = jnp.concatenate([segment_ids, jnp.full((KW - 1,), -1, jnp.int32)])
    inputs32 = layer_input.astype(jnp.float32)
    width = OUTPUT_CHANNELS // 8
    pieces = []
    for blk in range(8):
        cols = conv_grad[:, blk * width:(blk + 1) * width].astype(jnp.float32)
        padded = jnp.concatenate([cols, jnp.zeros((KW - 1, width), jnp.float32)], 0)
        total = conv_kernel[0, blk * width:(blk + 1) * width][None, :] * cols
        for offset in range(1, KW):
            same = pad_ids[offset:offset + TOKENS] == segment_ids
            term = conv_kernel[offset, blk * width:(blk + 1) * width][None, :] * padded[offset:offset + TOKENS]
            total = total + jnp.where(same[:, None], term, jnp.float32(0.0))
        channel = blk * width + jnp.arange(width, dtype=jnp.int32)
        convolved = (channel >= ZW) & (channel < ZW + XW)
        total = jnp.where(convolved[None, :], total, cols)
        proj_grad = total.astype(jnp.bfloat16).astype(jnp.float32)
        pieces.append(jnp.dot(inputs32.T, proj_grad, precision=upper_limit, preferred_element_type=jnp.float32))
    grad = jnp.concatenate(pieces, 1)
    blocks = grad.reshape(MODEL_WIDTH // BL, BL, OUTPUT_CHANNELS)
    left_term = jnp.einsum('bie,bje->bij', blocks, blocks, precision=upper_limit).reshape(MODEL_WIDTH, BL) / OUTPUT_CHANNELS
    column_bands = grad.reshape(MODEL_WIDTH, OUTPUT_CHANNELS // RIGHT_BLOCK_SIZE, RIGHT_BLOCK_SIZE)
    right_factor_term = jnp.einsum('rtz,rtk->tzk', column_bands, column_bands, precision=upper_limit).reshape(OUTPUT_CHANNELS, RIGHT_BLOCK_SIZE) / MODEL_WIDTH
    new_left_stat = 0.9 * left_stat + 0.1 * left_term
    new_right_stat = 0.9 * right_stat + 0.1 * right_factor_term
    left_q = left_basis.reshape(MODEL_WIDTH // BL, BL, BL)
    right_q = right_basis.reshape(OUTPUT_CHANNELS // RIGHT_BLOCK_SIZE, RIGHT_BLOCK_SIZE, RIGHT_BLOCK_SIZE)
    half = jnp.einsum('bki,bke->bie', left_q, blocks, precision=upper_limit).reshape(MODEL_WIDTH, OUTPUT_CHANNELS // RIGHT_BLOCK_SIZE, RIGHT_BLOCK_SIZE)
    rotated = jnp.einsum('dck,ckj->dcj', half, right_q, precision=upper_limit).reshape(MODEL_WIDTH, OUTPUT_CHANNELS)
    new_first = 0.9 * first_moment + 0.1 * rotated
    new_second = 0.95 * second_moment + 0.05 * rotated * rotated
    scaled = new_first / (jnp.sqrt(new_second) + 1e-08)
    back = jnp.einsum('bik,bke->bie', left_q, scaled.reshape(MODEL_WIDTH // BL, BL, OUTPUT_CHANNELS), precision=upper_limit).reshape(MODEL_WIDTH, OUTPUT_CHANNELS // RIGHT_BLOCK_SIZE, RIGHT_BLOCK_SIZE)
    direction = jnp.einsum('dck,cjk->dcj', back, right_q, precision=upper_limit).reshape(MODEL_WIDTH, OUTPUT_CHANNELS)
    return (new_left_stat, new_right_stat, new_first, new_second, direction)
```

```python
import jax
import jax.numpy as jnp
from jax import lax
from jax.experimental import pallas as pl
from jax.experimental.pallas import tpu as pltpu
from jax.sharding import PartitionSpec as P

MODEL_WIDTH = 3072
OUTPUT_CHANNELS = 13312
ZW = 6144
XW = 6656
TOK = 2048
FEAT = 384
CH = 1664
BL = 192
HALO = 16
F32 = jnp.float32
BF16 = jnp.bfloat16
MESH = pl.DeviceIdType.MESH

SIZES = (32, 32, 32, 32, 32, 16, 16)
XFIRST = (True, True, False, False, False, False, False)
OFFS = tuple(sum(SIZES[:i]) for i in range(len(SIZES)))
NCH = len(SIZES)


class Messages:
    def __init__(self, send_sems, recv_sems):
        self.send_sems, self.recv_sems = send_sems, recv_sems
        self.copies = []

    def make(self, src, dst, device):
        i = len(self.copies)
        copy = pltpu.make_async_remote_copy(
            src_ref=src,
            dst_ref=dst,
            send_sem=self.send_sems.at[i],
            recv_sem=self.recv_sems.at[i],
            device_id=device,
            device_id_type=MESH,
        )
        copy.start()
        self.copies.append(copy)
        return copy


def grad_kernel(x_hbm, cg_hbm, taps_ref, ids_ref, grad_ref, *scratch):
    (x_v, cg, proj, ids_col, ids_after, stage, xrecv, local_sems, send_sems, recv_sems) = scratch[:10]
    rest = scratch[10:]
    xt = rest[:NCH]
    zsend = rest[NCH : 2 * NCH]
    zrecv = rest[2 * NCH : 3 * NCH]
    zown = rest[3 * NCH : 4 * NCH]
    ysend = rest[4 * NCH : 5 * NCH]
    yrecv = rest[5 * NCH : 6 * NCH]

    row = lax.axis_index("row")
    col = lax.axis_index("col")
    y_hi, x = row // 4, row % 4
    y_lo, z, core = col // 8, (col // 2) % 4, col % 2
    r_left = y_hi * 4 + (x + 3) % 4
    r_right = y_hi * 4 + (x + 1) % 4
    r_far = y_hi * 4 + (x + 2) % 4

    def across(r):
        return (r + 4) % 8

    d_y = (across(row), col)
    d_right = (r_right, col)
    d_left = (r_left, col)
    d_sib = (row, y_lo * 8 + z * 2 + (1 - core))
    d_z = [(row, y_lo * 8 + ((z + k) % 4) * 2 + core) for k in (1, 2, 3)]
    d_ylo = (row, (1 - y_lo) * 8 + z * 2 + core)
    d_prev = (row, (col + 15) % 16)
    d_next = (row, (col + 1) % 16)

    load_x = pltpu.make_async_copy(x_hbm, x_v, local_sems.at[0])
    load_x.start()
    load_cg = pltpu.make_async_copy(cg_hbm, cg.at[pl.ds(0, TOK)], local_sems.at[1])
    load_cg.start()

    barrier = pltpu.get_barrier_semaphore()
    peers = [d_y, d_right, d_left, d_sib, *d_z, d_ylo, d_prev, d_next]
    for d in peers:
        pl.semaphore_signal(barrier, inc=1, device_id=d, device_id_type=MESH)

    load_x.wait()
    for b in range(3):
        turned = jnp.transpose(x_v[:, 128 * b : 128 * (b + 1)])
        for g in range(8):
            f = 128 * b + 16 * g
            half, within = f // BL, f % BL
            j = max(i for i in range(NCH) if OFFS[i] <= within)
            at = half * SIZES[j] + within - OFFS[j]
            xt[j][row, at : at + 16, :] = turned[16 * g : 16 * g + 16, :]
    pl.semaphore_wait(barrier, len(peers))

    msgs = Messages(send_sems, recv_sems)
    done = {}

    def slot(j, r):
        return xt[j].at[r]

    def send_own(j):
        done["xo", j] = [msgs.make(slot(j, row), slot(j, row), d) for d in (d_right, d_left)]

    def forward(j, key, out, left, right):
        n = SIZES[j]
        from_left, from_right = done[key, j]
        from_left.wait_recv()
        a = msgs.make(xt[j].at[left, pl.ds(0, n)], xt[j].at[left, pl.ds(0, n)], d_right)
        from_right.wait_recv()
        b = msgs.make(xt[j].at[right, pl.ds(n, n)], xt[j].at[right, pl.ds(n, n)], d_left)
        done[out, j] = [a, b]

    def forward_own(j):
        forward(j, "xo", "fo", r_left, r_right)

    def send_y(j):
        done["y", j] = [msgs.make(slot(j, row), slot(j, row), d_y)]

    def send_across(j):
        done["y", j][0].wait_recv()
        s = across(row)
        done["xq", j] = [msgs.make(slot(j, s), slot(j, s), d) for d in (d_right, d_left)]

    def forward_across(j):
        forward(j, "xq", "fq", across(r_left), across(r_right))

    def send_y_sides(j):
        done["y", j] += [msgs.make(slot(j, s), slot(j, s), d_y) for s in (r_left, r_right)]

    def send_y_far(j):
        for c in done["fo", j]:
            c.wait_recv()
        done["y", j] += [msgs.make(slot(j, r_far), slot(j, r_far), d_y)]

    def gathered(j):
        for c in done["y", j] if XFIRST[j] else done["fo", j] + done["fq", j]:
            c.wait_recv()

    order = []

    def multiply(j):
        n = SIZES[j]
        m = len(order)
        s = m % 2
        if m >= 2:
            done["ex", order[m - 2]].wait_send()
        lhs_ref = xt[j]

        def tile(cols, width):
            out = jnp.dot(
                lhs_ref[...].reshape(16 * n, TOK), proj[:, cols], preferred_element_type=F32
            ).reshape(8, 2, n, width)
            stage[s, 0, :, :n, cols] = out[:, 0]
            stage[s, 1, :, :n, cols] = out[:, 1]

        def step(i, _):
            tile(pl.ds(pl.multiple_of(i * 256, 256), 256), 256)
            return 0

        lax.fori_loop(0, CH // 256, step, 0)
        tile(pl.ds(CH // 256 * 256, CH % 256), CH % 256)
        order.append(j)

    def exchange(j):
        n = SIZES[j]
        s = order.index(j) % 2
        done["ex", j] = msgs.make(
            stage.at[s, 1 - core, :, pl.ds(0, n)], xrecv.at[s, :, pl.ds(0, n)], d_sib
        )

    def scatter_z(j):
        n = SIZES[j]
        s = order.index(j) % 2
        done["ex", j].wait_recv()
        done["z", j] = []
        for k in (2, 1, 3):
            for yl in range(2):
                at = yl * 4 + (z + k) % 4
                total = stage[s, core, at, :n] + xrecv[s, at, :n]
                zsend[j][k - 1, yl] = total.astype(BF16)
            done["z", j].append(msgs.make(zsend[j].at[k - 1], zrecv[j].at[k - 1], d_z[k - 1]))
        for yl in range(2):
            at = yl * 4 + z
            zown[j][yl] = stage[s, core, at, :n] + xrecv[s, at, :n]

    def scatter_y(j):
        n = SIZES[j]
        for c in done["z", j]:
            c.wait_recv()

        def total(yl):
            parts = [zrecv[j][k, yl].astype(F32) for k in range(3)]
            return (parts[0] + parts[1]) + (parts[2] + zown[j][yl])

        ysend[j][...] = total(1 - y_lo).astype(BF16)
        done["ys", j] = msgs.make(ysend[j], yrecv[j], d_ylo)
        grad_ref[OFFS[j] : OFFS[j] + n, :] = total(y_lo)

    def finish(j):
        n = SIZES[j]
        done["ys", j].wait_recv()
        rows = slice(OFFS[j], OFFS[j] + n)
        grad_ref[rows, :] = grad_ref[rows, :] + yrecv[j][...].astype(F32)

    channel = row * CH + lax.broadcasted_iota(jnp.int32, (1, CH), 1)
    convolved = (channel >= ZW) & (channel < ZW + XW)
    taps = [
        jnp.where(convolved, taps_ref[k : k + 1, :], F32(1.0 if k == 0 else 0.0)) for k in range(4)
    ]

    def number_columns():
        for q in range(TOK // 128):
            line = jnp.broadcast_to(ids_ref[q : q + 1, :].astype(F32), (128, 128))
            ids_col[128 * q : 128 * (q + 1), :] = jnp.transpose(line)

    def number_after():
        line = jnp.where(col == 15, F32(-1.0), ids_after[0:1, :].astype(F32))
        ids_col[TOK : TOK + HALO, :] = jnp.transpose(jnp.broadcast_to(line, (128, 128)))[:HALO]

    def convolve(first, last):
        rows = 64

        def step(i, _):
            t = pl.multiple_of(i * rows, rows)
            ids = ids_col[pl.ds(t, rows + HALO), :]
            same = [ids[k : k + rows] == ids[:rows] for k in range(1, 4)]
            for b in range(CH // 128):
                lanes = slice(128 * b, 128 * (b + 1))
                g = cg[pl.ds(t, rows + HALO), lanes].astype(F32)
                total = taps[0][:, lanes] * g[:rows]
                for k in range(1, 4):
                    term = taps[k][:, lanes] * g[k : k + rows]
                    total = total + jnp.where(same[k - 1], term, F32(0.0))
                proj[pl.ds(t, rows), lanes] = total.astype(BF16)
            return 0

        lax.fori_loop(first, last, step, 0)

    halo = [
        msgs.make(cg_hbm.at[pl.ds(0, HALO)], cg.at[pl.ds(TOK, HALO)], d_prev),
        msgs.make(ids_ref.at[pl.ds(0, 8)], ids_after, d_prev),
    ]
    A, B, C, D, E, F, G = range(7)
    send_own(A)
    send_y(C)
    send_own(B)
    send_y(A)
    send_own(C)
    send_y(D)
    send_y(B)
    number_columns()
    load_cg.wait()
    convolve(0, 16)
    forward_own(A)
    send_y_sides(A)
    send_across(C)
    forward_own(B)
    send_y(E)
    for c in halo:
        c.wait_recv()
    number_after()
    convolve(16, 32)
    send_own(D)
    send_y_far(A)
    forward_own(C)
    send_across(D)
    send_y_sides(B)
    send_y_far(B)
    send_y(F)
    send_y(G)
    forward_across(C)
    send_own(E)
    send_across(E)
    gathered(C)
    multiply(C)
    exchange(C)
    forward_own(D)
    gathered(A)
    multiply(A)
    forward_across(D)
    scatter_z(C)
    exchange(A)
    send_own(F)
    send_across(F)
    gathered(D)
    multiply(D)
    forward_own(E)
    scatter_z(A)
    exchange(D)
    scatter_y(C)
    gathered(B)
    multiply(B)
    forward_across(E)
    scatter_z(D)
    exchange(B)
    send_own(G)
    send_across(G)
    scatter_y(A)
    finish(C)
    forward_own(F)
    gathered(E)
    multiply(E)
    scatter_z(B)
    exchange(E)
    forward_across(F)
    scatter_y(D)
    finish(A)
    forward_own(G)
    scatter_z(E)
    forward_across(G)
    gathered(F)
    multiply(F)
    exchange(F)
    scatter_y(B)
    finish(D)
    gathered(G)
    multiply(G)
    scatter_z(F)
    exchange(G)
    scatter_y(E)
    scatter_z(G)
    finish(B)
    finish(E)
    scatter_y(F)
    scatter_y(G)
    finish(F)
    finish(G)
    waited = [done["ex", j] for j in order[:-2]]
    for c in msgs.copies:
        if not any(c is w for w in waited):
            c.wait_send()
    assert len(msgs.copies) <= NMSG


NMSG = 160


def per_chunk(shape, dtype):
    return [pltpu.VMEM(shape(n), dtype) for n in SIZES]


def gradient(layer_input, conv_grad, conv_kernel, segment_ids):
    top = max(SIZES)
    return pl.pallas_call(
        grad_kernel,
        out_shape=jax.ShapeDtypeStruct((BL, CH), F32),
        in_specs=[
            pl.BlockSpec(memory_space=pl.ANY),
            pl.BlockSpec(memory_space=pl.ANY),
            pl.BlockSpec(memory_space=pltpu.VMEM),
            pl.BlockSpec(memory_space=pltpu.VMEM),
        ],
        out_specs=pl.BlockSpec(memory_space=pltpu.VMEM),
        scratch_shapes=[
            pltpu.VMEM((TOK, FEAT), BF16),
            pltpu.VMEM((TOK + HALO, CH), BF16),
            pltpu.VMEM((TOK, CH), BF16),
            pltpu.VMEM((TOK + HALO, 128), F32),
            pltpu.VMEM((8, 128), jnp.int32),
            pltpu.VMEM((2, 2, 8, top, CH), F32),
            pltpu.VMEM((2, 8, top, CH), F32),
            pltpu.SemaphoreType.DMA((2,)),
            pltpu.SemaphoreType.DMA((NMSG,)),
            pltpu.SemaphoreType.DMA((NMSG,)),
            *per_chunk(lambda n: (8, 2 * n, TOK), BF16),
            *per_chunk(lambda n: (3, 2, n, CH), BF16),
            *per_chunk(lambda n: (3, 2, n, CH), BF16),
            *per_chunk(lambda n: (2, n, CH), F32),
            *per_chunk(lambda n: (n, CH), BF16),
            *per_chunk(lambda n: (n, CH), BF16),
        ],
        name="gradient",
        cost_estimate=pl.CostEstimate(
            flops=2 * MODEL_WIDTH * TOK * CH, bytes_accessed=10_000_000, transcendentals=0
        ),
        compiler_params=pltpu.CompilerParams(
            collective_id=0, has_side_effects=True, vmem_limit_bytes=62 << 20
        ),
    )(layer_input, conv_grad, conv_kernel, segment_ids.reshape(TOK // 128, 128))


def shards(
    layer_input,
    conv_grad,
    conv_kernel,
    segment_ids,
    left_basis,
    right_basis,
    left_stat,
    right_stat,
    first_moment,
    second_moment,
):
    highest_precision = lax.Precision.HIGHEST
    dcols = left_basis.shape[0]
    lblock = left_basis.shape[1]
    output_channel_columns = right_basis.shape[0]
    right_block_index = right_basis.shape[1]
    grad = gradient(layer_input, conv_grad, conv_kernel, segment_ids)
    nblocks = dcols // lblock
    nstrips = output_channel_columns // right_block_index
    blocks = grad.reshape(nblocks, lblock, output_channel_columns)
    left_term = (
        jnp.einsum("bie,bje->bij", blocks, blocks, precision=highest_precision).reshape(
            dcols, lblock
        )
        / OUTPUT_CHANNELS
    )
    column_bands = grad.reshape(dcols, nstrips, right_block_index)
    right_factor_term = (
        jnp.einsum("rtz,rtk->tzk", column_bands, column_bands, precision=highest_precision).reshape(
            output_channel_columns, right_block_index
        )
        / MODEL_WIDTH
    )
    left_sum = lax.psum(left_term.astype(jnp.bfloat16), "row").astype(jnp.float32)
    right_sum = lax.psum(right_factor_term.astype(jnp.bfloat16), "col").astype(jnp.float32)
    lwidth = left_stat.shape[1]
    rwidth = right_stat.shape[1]
    left_part = lax.dynamic_slice_in_dim(left_sum, lax.axis_index("row") * lwidth, lwidth, 1)
    right_part = lax.dynamic_slice_in_dim(right_sum, lax.axis_index("col") * rwidth, rwidth, 1)
    new_left_stat = 0.9 * left_stat + 0.1 * left_part
    new_right_stat = 0.9 * right_stat + 0.1 * right_part
    left_q = left_basis.reshape(nblocks, lblock, lblock)
    right_q = right_basis.reshape(nstrips, right_block_index, right_block_index)
    half = jnp.einsum("bki,bke->bie", left_q, blocks, precision=highest_precision).reshape(
        dcols, nstrips, right_block_index
    )
    rotated = jnp.einsum("dck,ckj->dcj", half, right_q, precision=highest_precision).reshape(
        dcols, output_channel_columns
    )
    new_first = 0.9 * first_moment + 0.1 * rotated
    new_second = 0.95 * second_moment + 0.05 * rotated * rotated
    scaled = new_first / (jnp.sqrt(new_second) + 1e-08)
    back = jnp.einsum(
        "bik,bke->bie",
        left_q,
        scaled.reshape(nblocks, lblock, output_channel_columns),
        precision=highest_precision,
    ).reshape(dcols, nstrips, right_block_index)
    direction = jnp.einsum("dck,cjk->dcj", back, right_q, precision=highest_precision).reshape(
        dcols, output_channel_columns
    )
    return (new_left_stat, new_right_stat, new_first, new_second, direction)


def solution(mesh):
    placed = (
        P("col", "row"),
        P("col", "row"),
        P(None, "row"),
        P("col"),
        P("col", None),
        P("row", None),
        P("col", "row"),
        P("row", "col"),
        P("col", "row"),
        P("col", "row"),
    )
    return jax.shard_map(
        shards,
        mesh=mesh,
        in_specs=placed,
        out_specs=(
            P("col", "row"),
            P("row", "col"),
            P("col", "row"),
            P("col", "row"),
            P("col", "row"),
        ),
        check_vma=False,
    )
```

```python
import jax
import jax.numpy as jnp
from jax import lax
from jax.experimental import pallas as pl
from jax.experimental.pallas import tpu as pltpu
from jax.sharding import PartitionSpec as P

MODEL_WIDTH = 3072
OUTPUT_CHANNELS = 13312
ZW = 6144
XW = 6656
TOK = 2048
FEAT = 384
CH = 1664
BL = 192
HALO = 16
F32 = jnp.float32
BF16 = jnp.bfloat16
MESH = pl.DeviceIdType.MESH

SIZES = (32, 32, 32, 32, 32, 16, 16)
XFIRST = (True, True, False, False, False, False, False)
OFFS = tuple(sum(SIZES[:i]) for i in range(len(SIZES)))
NCH = len(SIZES)
GRAM = NCH
ROWS = SIZES + (32,)
STRIPS = 4
RB = 416
RSHARE = 26
LSHARE = 24
NFIX = 20


def contract(a, b, da, db):
    return lax.dot_general(a, b, (((da,), (db,)), ((), ())), preferred_element_type=F32)


def split(v):
    high = v.astype(BF16)
    return high, (v - high.astype(F32)).astype(BF16)


def contract3(a, b, da, db):
    small = contract(a[0], b[1], da, db) + contract(a[1], b[0], da, db)
    return contract(a[0], b[0], da, db) + small


class Messages:
    def __init__(self, send_sems, recv_sems):
        self.send_sems, self.recv_sems = send_sems, recv_sems
        self.copies = []

    def make(self, src, dst, device):
        i = len(self.copies)
        copy = pltpu.make_async_remote_copy(
            src_ref=src,
            dst_ref=dst,
            send_sem=self.send_sems.at[i],
            recv_sem=self.recv_sems.at[i],
            device_id=device,
            device_id_type=MESH,
        )
        copy.start()
        self.copies.append(copy)
        return copy


def step_kernel(
    x_hbm, cg_hbm, right_basis_hbm, right_stat_hbm, first_hbm, second_hbm,
    taps_ref, ids_ref, left_basis_ref, left_stat_ref,
    first_out, second_out, direction_out, new_left_ref, new_right_ref,
    *scratch,
):
    (x_v, cg, proj, ids_col, ids_after, stage, xrecv, grad_ref, first, second, work, gram,
     right_basis, right_stat, left_send, left_recv, left_gram,
     local_sems, send_sems, recv_sems) = scratch[:NFIX]
    rest = scratch[NFIX:]
    xt = rest[:NCH]
    zsend, zrecv, zown, ysend, yrecv = [
        rest[NCH + i * (NCH + 1) : NCH + (i + 1) * (NCH + 1)] for i in range(5)
    ]

    row = lax.axis_index("row")
    col = lax.axis_index("col")
    y_hi, x = row // 4, row % 4
    y_lo, z, core = col // 8, (col // 2) % 4, col % 2
    r_left = y_hi * 4 + (x + 3) % 4
    r_right = y_hi * 4 + (x + 1) % 4
    r_far = y_hi * 4 + (x + 2) % 4

    def across(r):
        return (r + 4) % 8

    d_y = (across(row), col)
    d_right = (r_right, col)
    d_left = (r_left, col)
    d_sib = (row, y_lo * 8 + z * 2 + (1 - core))
    d_z = [(row, y_lo * 8 + ((z + k) % 4) * 2 + core) for k in (1, 2, 3)]
    d_ylo = (row, (1 - y_lo) * 8 + z * 2 + core)
    d_prev = (row, (col + 15) % 16)
    d_next = (row, (col + 1) % 16)

    load_x = pltpu.make_async_copy(x_hbm, x_v, local_sems.at[0])
    load_x.start()
    load_cg = pltpu.make_async_copy(cg_hbm, cg.at[pl.ds(0, TOK)], local_sems.at[1])
    load_cg.start()

    later_loads = [
        pltpu.make_async_copy(src, dst, local_sems.at[2 + i])
        for i, (src, dst) in enumerate(
            [
                (right_basis_hbm, right_basis),
                (first_hbm, first),
                (second_hbm, second),
                (right_stat_hbm, right_stat),
            ]
        )
    ]

    barrier = pltpu.get_barrier_semaphore()
    d_row = [((row + k) % 8, col) for k in range(1, 8)]
    peers = [*d_row, d_sib, *d_z, d_ylo, d_prev, d_next]
    for d in peers:
        pl.semaphore_signal(barrier, inc=1, device_id=d, device_id_type=MESH)

    load_x.wait()
    for b in range(3):
        turned = jnp.transpose(x_v[:, 128 * b : 128 * (b + 1)])
        for g in range(8):
            f = 128 * b + 16 * g
            half, within = f // BL, f % BL
            j = max(i for i in range(NCH) if OFFS[i] <= within)
            at = half * ROWS[j] + within - OFFS[j]
            xt[j][row, at : at + 16, :] = turned[16 * g : 16 * g + 16, :]
    pl.semaphore_wait(barrier, len(peers))

    msgs = Messages(send_sems, recv_sems)
    done = {}

    def slot(j, r):
        return xt[j].at[r]

    def send_own(j):
        done["xo", j] = [msgs.make(slot(j, row), slot(j, row), d) for d in (d_right, d_left)]

    def forward(j, key, out, left, right):
        n = ROWS[j]
        from_left, from_right = done[key, j]
        from_left.wait_recv()
        a = msgs.make(xt[j].at[left, pl.ds(0, n)], xt[j].at[left, pl.ds(0, n)], d_right)
        from_right.wait_recv()
        b = msgs.make(xt[j].at[right, pl.ds(n, n)], xt[j].at[right, pl.ds(n, n)], d_left)
        done[out, j] = [a, b]

    def forward_own(j):
        forward(j, "xo", "fo", r_left, r_right)

    def send_y(j):
        done["y", j] = [msgs.make(slot(j, row), slot(j, row), d_y)]

    def send_across(j):
        done["y", j][0].wait_recv()
        s = across(row)
        done["xq", j] = [msgs.make(slot(j, s), slot(j, s), d) for d in (d_right, d_left)]

    def forward_across(j):
        forward(j, "xq", "fq", across(r_left), across(r_right))

    def send_y_sides(j):
        done["y", j] += [msgs.make(slot(j, s), slot(j, s), d_y) for s in (r_left, r_right)]

    def send_y_far(j):
        for c in done["fo", j]:
            c.wait_recv()
        done["y", j] += [msgs.make(slot(j, r_far), slot(j, r_far), d_y)]

    def gathered(j):
        for c in done["y", j] if XFIRST[j] else done["fo", j] + done["fq", j]:
            c.wait_recv()

    order = []

    def multiply(j):
        n = ROWS[j]
        m = len(order)
        s = m % 2
        if m >= 2:
            done["ex", order[m - 2]].wait_send()
        lhs_ref = xt[j]

        def tile(cols, width):
            out = jnp.dot(
                lhs_ref[...].reshape(16 * n, TOK), proj[:, cols], preferred_element_type=F32
            ).reshape(8, 2, n, width)
            stage[s, 0, :, :n, cols] = out[:, 0]
            stage[s, 1, :, :n, cols] = out[:, 1]

        def step(i, _):
            tile(pl.ds(pl.multiple_of(i * 256, 256), 256), 256)
            return 0

        lax.fori_loop(0, CH // 256, step, 0)
        tile(pl.ds(CH // 256 * 256, CH % 256), CH % 256)
        order.append(j)

    def exchange(j):
        n = ROWS[j]
        s = order.index(j) % 2
        done["ex", j] = msgs.make(
            stage.at[s, 1 - core, :, pl.ds(0, n)], xrecv.at[s, :, pl.ds(0, n)], d_sib
        )

    def scatter_z(j):
        n = ROWS[j]
        s = order.index(j) % 2
        done["ex", j].wait_recv()
        done["z", j] = []
        for k in (2, 1, 3):
            for yl in range(2):
                at = yl * 4 + (z + k) % 4
                total = stage[s, core, at, :n] + xrecv[s, at, :n]
                zsend[j][k - 1, yl] = total.astype(BF16)
            done["z", j].append(msgs.make(zsend[j].at[k - 1], zrecv[j].at[k - 1], d_z[k - 1]))
        for yl in range(2):
            at = yl * 4 + z
            zown[j][yl] = stage[s, core, at, :n] + xrecv[s, at, :n]

    def scatter_y(j):
        n = ROWS[j]
        for c in done["z", j]:
            c.wait_recv()

        def total(yl):
            parts = [zrecv[j][k, yl].astype(F32) for k in range(3)]
            return (parts[0] + parts[1]) + (parts[2] + zown[j][yl])

        ysend[j][...] = total(1 - y_lo).astype(BF16)
        done["ys", j] = msgs.make(ysend[j], yrecv[j], d_ylo)
        if j == GRAM:
            gram[...] = total(y_lo)
        else:
            grad_ref[OFFS[j] : OFFS[j] + n, :] = total(y_lo)

    def finish(j):
        n = ROWS[j]
        done["ys", j].wait_recv()
        if j == GRAM:
            gram[...] = gram[...] + yrecv[j][...].astype(F32)
            return
        rows = slice(OFFS[j], OFFS[j] + n)
        grad_ref[rows, :] = grad_ref[rows, :] + yrecv[j][...].astype(F32)

    channel = row * CH + lax.broadcasted_iota(jnp.int32, (1, CH), 1)
    convolved = (channel >= ZW) & (channel < ZW + XW)
    taps = [
        jnp.where(convolved, taps_ref[k : k + 1, :], F32(1.0 if k == 0 else 0.0)) for k in range(4)
    ]

    def number_columns():
        for q in range(TOK // 128):
            line = jnp.broadcast_to(ids_ref[q : q + 1, :].astype(F32), (128, 128))
            ids_col[128 * q : 128 * (q + 1), :] = jnp.transpose(line)

    def number_after():
        line = jnp.where(col == 15, F32(-1.0), ids_after[0:1, :].astype(F32))
        ids_col[TOK : TOK + HALO, :] = jnp.transpose(jnp.broadcast_to(line, (128, 128)))[:HALO]

    def convolve(first, last):
        rows = 64

        def step(i, _):
            t = pl.multiple_of(i * rows, rows)
            ids = ids_col[pl.ds(t, rows + HALO), :]
            same = [ids[k : k + rows] == ids[:rows] for k in range(1, 4)]
            for b in range(CH // 128):
                lanes = slice(128 * b, 128 * (b + 1))
                g = cg[pl.ds(t, rows + HALO), lanes].astype(F32)
                total = taps[0][:, lanes] * g[:rows]
                for k in range(1, 4):
                    term = taps[k][:, lanes] * g[k : k + rows]
                    total = total + jnp.where(same[k - 1], term, F32(0.0))
                proj[pl.ds(t, rows), lanes] = total.astype(BF16)
            return 0

        lax.fori_loop(first, last, step, 0)

    def strip(t):
        return slice(RB * t, RB * (t + 1))

    def q_right(t):
        return cg[strip(t), :RB], cg[strip(t), 512 : 512 + RB]

    halo = [
        msgs.make(cg_hbm.at[pl.ds(0, HALO)], cg.at[pl.ds(TOK, HALO)], d_prev),
        msgs.make(ids_ref.at[pl.ds(0, 8)], ids_after, d_prev),
    ]
    A, B, C, D, E, F, G = range(7)
    send_own(A)
    send_y(C)
    send_own(B)
    send_y(A)
    send_own(C)
    send_y(D)
    send_y(B)
    for c in later_loads:
        c.start()
    number_columns()
    load_cg.wait()
    convolve(0, 16)
    forward_own(A)
    send_y_sides(A)
    send_across(C)
    forward_own(B)
    send_y(E)
    for c in halo:
        c.wait_recv()
    number_after()
    convolve(16, 32)
    for c in later_loads:
        c.wait()
    for t in range(STRIPS):
        high, low = split(right_basis[strip(t), :])
        cg[strip(t), :RB] = high
        cg[strip(t), 512 : 512 + RB] = low
    send_own(D)
    send_y_far(A)
    forward_own(C)
    send_across(D)
    send_y_sides(B)
    send_y_far(B)
    send_y(F)
    send_y(G)
    forward_across(C)
    send_own(E)
    send_across(E)
    gathered(C)
    multiply(C)
    exchange(C)
    forward_own(D)
    gathered(A)
    multiply(A)
    forward_across(D)
    scatter_z(C)
    exchange(A)
    send_own(F)
    send_across(F)
    gathered(D)
    multiply(D)
    forward_own(E)
    scatter_z(A)
    exchange(D)
    scatter_y(C)
    gathered(B)
    multiply(B)
    forward_across(E)
    scatter_z(D)
    exchange(B)
    send_own(G)
    send_across(G)
    scatter_y(A)
    finish(C)
    forward_own(F)
    gathered(E)
    multiply(E)
    scatter_z(B)
    exchange(E)
    forward_across(F)
    scatter_y(D)
    finish(A)
    forward_own(G)
    scatter_z(E)
    forward_across(G)
    gathered(F)
    multiply(F)
    exchange(F)
    scatter_y(B)
    finish(D)
    gathered(G)
    multiply(G)
    scatter_z(F)
    exchange(G)
    scatter_y(E)
    scatter_z(G)
    finish(B)
    finish(E)
    scatter_y(F)
    scatter_y(G)
    finish(F)
    finish(G)

    place = lax.broadcasted_iota(jnp.int32, (RB, 16 * 32), 1)
    source = lax.broadcasted_iota(jnp.int32, (RB, 16 * 32), 0)
    chosen = (place % 32 < RSHARE) & (place // 32 * RSHARE + place % 32 == source)
    one_hot = jnp.where(chosen, F32(1.0), F32(0.0)).astype(BF16)
    slot_gram = len(order) % 2
    done["ex", order[-2]].wait_send()
    for t in range(STRIPS):
        band = grad_ref[:, strip(t)].astype(BF16)
        placed = jnp.dot(band, one_hot, preferred_element_type=F32).astype(BF16)
        block = contract(placed, band, 0, 0).reshape(8, 2, 32, RB)
        stage[slot_gram, 0, :, :, strip(t)] = block[:, 0]
        stage[slot_gram, 1, :, :, strip(t)] = block[:, 1]
    order.append(GRAM)
    exchange(GRAM)

    rounded = grad_ref[...].astype(BF16)
    left = contract(rounded, rounded, 1, 1)
    for r in range(8):
        share = left[LSHARE * r : LSHARE * (r + 1)]
        left_gram[r] = share
        padded = jnp.concatenate([share, jnp.zeros((32 - LSHARE, BL), F32)], 0)
        left_send[r] = padded.astype(BF16)
    left_copies = [
        msgs.make(left_send.at[(row + k) % 8], left_recv.at[k - 1], d_row[k - 1])
        for k in range(1, 8)
    ]

    q_left = split(left_basis_ref[...])
    work[...] = contract3(q_left, split(grad_ref[...]), 0, 0)
    scatter_z(GRAM)
    for t in range(STRIPS):
        rotated = contract3(split(work[:, strip(t)]), q_right(t), 1, 0)
        new_first = 0.9 * first[:, strip(t)] + 0.1 * rotated
        new_second = 0.95 * second[:, strip(t)] + 0.05 * rotated * rotated
        first[:, strip(t)] = new_first
        second[:, strip(t)] = new_second
        work[:, strip(t)] = new_first / (jnp.sqrt(new_second) + 1e-08)
    stores = [
        pltpu.make_async_copy(first, first_out, local_sems.at[6]),
        pltpu.make_async_copy(second, second_out, local_sems.at[7]),
        pltpu.make_async_copy(grad_ref, direction_out, local_sems.at[8]),
    ]
    stores[0].start()
    stores[1].start()
    work[...] = contract3(q_left, split(work[...]), 1, 0)
    for t in range(STRIPS):
        grad_ref[:, strip(t)] = contract3(split(work[:, strip(t)]), q_right(t), 1, 1)
    stores[2].start()

    for c in left_copies:
        c.wait_recv()
    total = jnp.concatenate([left_gram[row], jnp.zeros((32 - LSHARE, BL), F32)], 0)
    for k in range(7):
        total = total + left_recv[k].astype(F32)
    total = jnp.concatenate([total, jnp.zeros((32, 256 - BL), F32)], 1)
    total = jnp.concatenate([total, jnp.zeros((96, 256), F32)], 0)
    turned = jnp.transpose(total)[:BL, :LSHARE]
    new_left_ref[...] = 0.9 * left_stat_ref[...] + 0.1 * (turned / OUTPUT_CHANNELS)

    scatter_y(GRAM)
    finish(GRAM)
    for b in range(CH // 128):
        at = slice(128 * b, 128 * (b + 1))
        block = jnp.concatenate([gram[:, at], jnp.zeros((96, 128), F32)], 0)
        turned = jnp.transpose(block)[:, :RSHARE]
        new_right_ref[at, :] = 0.9 * right_stat[at, :] + 0.1 * (turned / MODEL_WIDTH)
    for c in stores:
        c.wait()
    waited = [done["ex", j] for j in order[:-2]]
    for c in msgs.copies:
        if not any(c is w for w in waited):
            c.wait_send()
    assert len(msgs.copies) <= NMSG


NMSG = 160


def shards(
    layer_input,
    conv_grad,
    conv_kernel,
    segment_ids,
    left_basis,
    right_basis,
    left_stat,
    right_stat,
    first_moment,
    second_moment,
):
    top = max(ROWS)
    any_spec = pl.BlockSpec(memory_space=pl.ANY)
    vmem = pl.BlockSpec(memory_space=pltpu.VMEM)
    block = jax.ShapeDtypeStruct((BL, CH), F32)

    def per_chunk(sizes, shape, dtype):
        return [pltpu.VMEM(shape(n), dtype) for n in sizes]

    first, second, direction, new_left, new_right = pl.pallas_call(
        step_kernel,
        out_shape=[
            block,
            block,
            block,
            jax.ShapeDtypeStruct((BL, LSHARE), F32),
            jax.ShapeDtypeStruct((CH, RSHARE), F32),
        ],
        in_specs=[any_spec] * 6 + [vmem] * 4,
        out_specs=[any_spec] * 3 + [vmem] * 2,
        scratch_shapes=[
            pltpu.VMEM((TOK, FEAT), BF16),
            pltpu.VMEM((TOK + HALO, CH), BF16),
            pltpu.VMEM((TOK, CH), BF16),
            pltpu.VMEM((TOK + HALO, 128), F32),
            pltpu.VMEM((8, 128), jnp.int32),
            pltpu.VMEM((2, 2, 8, top, CH), F32),
            pltpu.VMEM((2, 8, top, CH), F32),
            pltpu.VMEM((BL, CH), F32),
            pltpu.VMEM((BL, CH), F32),
            pltpu.VMEM((BL, CH), F32),
            pltpu.VMEM((BL, CH), F32),
            pltpu.VMEM((32, CH), F32),
            pltpu.VMEM((CH, RB), F32),
            pltpu.VMEM((CH, RSHARE), F32),
            pltpu.VMEM((8, 32, BL), BF16),
            pltpu.VMEM((7, 32, BL), BF16),
            pltpu.VMEM((8, LSHARE, BL), F32),
            pltpu.SemaphoreType.DMA((9,)),
            pltpu.SemaphoreType.DMA((NMSG,)),
            pltpu.SemaphoreType.DMA((NMSG,)),
            *per_chunk(SIZES, lambda n: (8, 2 * n, TOK), BF16),
            *per_chunk(ROWS, lambda n: (3, 2, n, CH), BF16),
            *per_chunk(ROWS, lambda n: (3, 2, n, CH), BF16),
            *per_chunk(ROWS, lambda n: (2, n, CH), F32),
            *per_chunk(ROWS, lambda n: (n, CH), BF16),
            *per_chunk(ROWS, lambda n: (n, CH), BF16),
        ],
        name="step",
        cost_estimate=pl.CostEstimate(
            flops=2 * MODEL_WIDTH * TOK * CH, bytes_accessed=20_000_000, transcendentals=0
        ),
        compiler_params=pltpu.CompilerParams(
            collective_id=0, has_side_effects=True, vmem_limit_bytes=63 << 20
        ),
    )(
        layer_input,
        conv_grad,
        right_basis,
        right_stat,
        first_moment,
        second_moment,
        conv_kernel,
        segment_ids.reshape(TOK // 128, 128),
        left_basis,
        left_stat,
    )
    return new_left, new_right, first, second, direction


def solution(mesh):
    placed = (
        P("col", "row"),
        P("col", "row"),
        P(None, "row"),
        P("col"),
        P("col", None),
        P("row", None),
        P("col", "row"),
        P("row", "col"),
        P("col", "row"),
        P("col", "row"),
    )
    return jax.shard_map(
        shards,
        mesh=mesh,
        in_specs=placed,
        out_specs=(
            P("col", "row"),
            P("row", "col"),
            P("col", "row"),
            P("col", "row"),
            P("col", "row"),
        ),
        check_vma=False,
    )
```

```python
import jax
import jax.numpy as jnp
from jax import lax
from jax.experimental import pallas as pl
from jax.experimental.pallas import tpu as pltpu
from jax.sharding import PartitionSpec as P

MODEL_WIDTH = 3072
OUTPUT_CHANNELS = 13312
ZW = 6144
XW = 6656
TOK = 2048
FEAT = 384
CH = 1664
BL = 192
RB = 416
STRIPS = 4
RSHARE = 26
LSHARE = 24
HALO = 16
F32 = jnp.float32
BF16 = jnp.bfloat16
MESH = pl.DeviceIdType.MESH

N = 16
NCH = BL // N
GRAMS = (NCH, NCH + 1)
NALL = NCH + 2
SLOTS = 4
XFIRST = (False, False, True, True, True, False, False, True, False, False, False, False)
ORDER = (
    ("xo", 0), ("xo", 1), ("y", 0), ("y", 1), ("y", 2), ("conv", 0), ("xo", 2), ("y", 3),
    ("conv", 1), ("fo", 0), ("xq", 0), ("y", 4), ("conv", 2), ("fo", 1), ("y", 5), ("xq", 1),
    ("conv", 3), ("fo", 2), ("ys", 2), ("xo", 3), ("fq", 0), ("y", 6), ("xo", 4), ("fq", 1),
    ("y", 8), ("xq", 5), ("yf", 2), ("fo", 3), ("mul", 0), ("xo", 5), ("ys", 3), ("fo", 4),
    ("ex", 0), ("mul", 1), ("xq", 6), ("ex", 1), ("sz", 0), ("fq", 5), ("ys", 4), ("mul", 2),
    ("fo", 5), ("ex", 2), ("sz", 1), ("xq", 8), ("yf", 3), ("sy", 0), ("sz", 2), ("xo", 6),
    ("fq", 6), ("yf", 4), ("mul", 5), ("xo", 7), ("y", 7), ("ex", 5), ("sy", 1), ("fq", 8),
    ("mul", 3), ("fo", 6), ("xo", 8), ("y", 9), ("ex", 3), ("sz", 5), ("y", 10), ("sy", 2),
    ("fin", 0), ("mul", 4), ("fo", 7), ("xo", 9), ("ex", 4), ("sz", 3), ("ys", 7), ("fin", 1),
    ("mul", 6), ("xq", 9), ("ex", 6), ("sz", 4), ("fo", 8), ("sy", 5), ("xo", 10), ("sz", 6),
    ("yf", 7), ("sy", 3), ("fo", 9), ("fin", 2), ("xq", 10), ("fq", 9), ("y", 11), ("sy", 4),
    ("mul", 8), ("xo", 11), ("ex", 8), ("fin", 5), ("fo", 10), ("sy", 6), ("mul", 7),
    ("fq", 10), ("ex", 7), ("sz", 8), ("fin", 3), ("mul", 9), ("xq", 11), ("ex", 9), ("sz", 7),
    ("fo", 11), ("fin", 4), ("fin", 6), ("mul", 10), ("ex", 10), ("sz", 9), ("fq", 11),
    ("sy", 8), ("mulp", "near"), ("exp", "near"), ("sz", 10), ("mulp", "far"), ("exp", "far"),
    ("sy", 7), ("scp", "near"), ("sy", 9), ("fin", 8), ("scp", "far"), ("fin", 7), ("sy", 10),
    ("fin", 9), ("fin", 10),
)
POOL = 40
NGROUP = 100
LAST = NCH - 1


def contract(a, b, da, db):
    return lax.dot_general(a, b, (((da,), (db,)), ((), ())), preferred_element_type=F32)


def split(v):
    high = v.astype(BF16)
    return high, (v - high.astype(F32)).astype(BF16)


def contract3(a, b, da, db):
    small = contract(a[0], b[1], da, db) + contract(a[1], b[0], da, db)
    return contract(a[0], b[0], da, db) + small


class Messages:
    def __init__(self, send_sems, recv_sems):
        self.send_sems, self.recv_sems = send_sems, recv_sems
        self.copies = []
        self.groups = {}
        self.sent = set()
        self.arrived = set()

    def make(self, key, src, dst, device):
        i = len(self.copies)
        if i >= POOL:
            self.release(i - POOL)
        group = self.groups.setdefault(key, len(self.groups))
        assert group < NGROUP
        copy = pltpu.make_async_remote_copy(
            src_ref=src,
            dst_ref=dst,
            send_sem=self.send_sems.at[i % POOL],
            recv_sem=self.recv_sems.at[group],
            device_id=device,
            device_id_type=MESH,
        )
        copy.start()
        self.copies.append(copy)
        return i

    def release(self, i):
        if i not in self.sent:
            self.sent.add(i)
            self.copies[i].wait_send()

    def arrive(self, key, like, device):
        if key not in self.arrived:
            self.arrived.add(key)
            pltpu.make_async_remote_copy(
                src_ref=like,
                dst_ref=like,
                send_sem=self.send_sems.at[0],
                recv_sem=self.recv_sems.at[self.groups[key]],
                device_id=device,
                device_id_type=MESH,
            ).wait_recv()


def step_kernel(
    x_hbm, cg_hbm, taps_hbm, ids_hbm, right_basis_hbm, first_hbm, second_hbm, right_stat_hbm,
    left_basis_hbm, left_stat_hbm,
    first_out, second_out, direction_out, new_left_out, new_right_out,
    *scratch,
):
    (x_v, cg, taps_ref, ids_ref, proj, ids_col, ids_after, xt, stage, xrecv, zsend, zrecv, zown,
     ysend, yrecv, qsend, qrecv, qown, gsend, grecv, dsend, drecv, grad_ref, first, second, work,
     right_basis, right_stat, left_basis, left_stat, left_send, left_recv,
     local_sems, send_sems, recv_sems, dsend_sems, drecv_sems) = scratch

    row = lax.axis_index("row")
    col = lax.axis_index("col")
    y_hi, x = row // 4, row % 4
    y_lo, z, core = col // 8, (col // 2) % 4, col % 2
    r_left = y_hi * 4 + (x + 3) % 4
    r_right = y_hi * 4 + (x + 1) % 4
    r_far = y_hi * 4 + (x + 2) % 4

    def across(r):
        return (r + 4) % 8

    d_row = [((row + k) % 8, col) for k in range(1, 8)]
    d_y = (across(row), col)
    d_right = (r_right, col)
    d_left = (r_left, col)
    d_sib = (row, y_lo * 8 + z * 2 + (1 - core))
    d_z = [(row, y_lo * 8 + ((z + k) % 4) * 2 + core) for k in (1, 2, 3)]
    d_ylo = (row, (1 - y_lo) * 8 + z * 2 + core)
    d_prev = (row, (col + 15) % 16)
    d_next = (row, (col + 1) % 16)

    barrier = pltpu.get_barrier_semaphore()
    peers = [*d_row, d_sib, *d_z, d_ylo, d_prev, d_next]
    for d in peers:
        pl.semaphore_signal(barrier, inc=1, device_id=d, device_id_type=MESH)

    loads = [
        pltpu.make_async_copy(src, dst, local_sems.at[i])
        for i, (src, dst) in enumerate(
            [
                (x_hbm, x_v),
                (cg_hbm, cg.at[pl.ds(0, TOK)]),
                (taps_hbm, taps_ref),
                (ids_hbm, ids_ref),
                (right_basis_hbm, right_basis),
                (first_hbm, first),
                (second_hbm, second),
                (right_stat_hbm, right_stat),
                (left_basis_hbm, left_basis),
                (left_stat_hbm, left_stat),
            ]
        )
    ]
    load_x, early_loads, later_loads = loads[0], loads[1:4], loads[4:]
    load_x.start()
    for c in early_loads:
        c.start()
    load_x.wait()
    for b in range(3):
        turned = jnp.transpose(x_v[:, 128 * b : 128 * (b + 1)])
        for g in range(8):
            at = 8 * b + g
            xt[at % NCH, row, N * (at // NCH) : N * (at // NCH + 1), :] = turned[
                N * g : N * (g + 1), :
            ]
    pl.semaphore_wait(barrier, len(peers))

    msgs = Messages(send_sems, recv_sems)
    done = {}

    rel = [row, r_left, r_right, across(row), across(r_left), across(r_right), r_far, across(r_far)]

    def send(kind, j, r, device):
        msgs.make((kind, j), xt.at[j, r], xt.at[j, r], device)

    def sent_round(kind, j):
        msgs.arrive((kind, j), xt.at[j, pl.ds(0, 2)], d_right)

    def forward(kind, out, j, left, right):
        sent_round(kind, j)
        half_a, half_b = xt.at[j, left, pl.ds(0, N)], xt.at[j, right, pl.ds(N, N)]
        msgs.make((out, j), half_a, half_a, d_right)
        msgs.make((out, j), half_b, half_b, d_left)

    def send_own(j):
        send("xo", j, row, d_right)
        send("xo", j, row, d_left)

    def forward_own(j):
        forward("xo", "fo" if XFIRST[j] else "far", j, r_left, r_right)

    def send_y(j):
        send("y", j, row, d_y)

    def send_across(j):
        msgs.arrive(("y", j), xt.at[j, 0], d_y)
        send("xq", j, across(row), d_right)
        send("xq", j, across(row), d_left)

    def forward_across(j):
        forward("xq", "far", j, across(r_left), across(r_right))

    def send_y_sides(j):
        sent_round("xo", j)
        send("y", j, r_left, d_y)
        send("y", j, r_right, d_y)

    def send_y_far(j):
        msgs.arrive(("fo", j), xt.at[j, 0], d_right)
        send("y", j, r_far, d_y)

    def gathered(j):
        if XFIRST[j]:
            msgs.arrive(("y", j), xt.at[j, pl.ds(0, 4)], d_y)
        else:
            msgs.arrive(("far", j), xt.at[j, pl.ds(0, 2)], d_right)

    products = []
    exchanged = {}
    added = set()

    def place_in_stage(j):
        m = len(products)
        if m >= SLOTS:
            assert products[m - SLOTS] in added
            for i in exchanged[products[m - SLOTS]]:
                msgs.release(i)
        products.append(j)
        return m % SLOTS

    def over_tiles(tile):
        def step(i, _):
            tile(pl.ds(pl.multiple_of(i * 512, 512), 512), 512)
            return 0

        lax.fori_loop(0, CH // 512, step, 0)
        tile(pl.ds(CH // 512 * 512, CH % 512), CH % 512)

    def multiply(j):
        gathered(j)
        s = place_in_stage(j)

        def tile(cols, width):
            out = jnp.dot(
                xt[j].reshape(16 * N, TOK), proj[:, cols], preferred_element_type=F32
            ).reshape(8, 2, N, width)
            stage[s, 0, :, :, cols] = out[:, 0]
            stage[s, 1, :, :, cols] = out[:, 1]

        over_tiles(tile)

    def may_exchange(j):
        m = products.index(j)
        assert m < 2 or products[m - 2] in added
        return m % SLOTS

    def exchange(j):
        s = may_exchange(j)
        exchanged[j] = [msgs.make(("ex", j), stage.at[s, 1 - core], xrecv.at[s], d_sib)]

    def take_exchange(j):
        msgs.arrive(("ex", j), xrecv.at[0], d_sib)
        added.add(j)

    def both_cores(j, at):
        s = products.index(j) % SLOTS
        if j in GRAMS:
            return stage[s, 0, at] + grecv[j - NCH, at].astype(F32)
        return stage[s, core, at] + xrecv[s, at]

    def scatter_z(j):
        if j < NCH:
            take_exchange(j)
        for k in (2, 1, 3):
            for yl in range(2):
                zsend[j, k - 1, yl] = both_cores(j, yl * 4 + (z + k) % 4).astype(BF16)
            msgs.make(("z", j), zsend.at[j, k - 1], zrecv.at[j, k - 1], d_z[k - 1])
        for yl in range(2):
            zown[j, yl] = both_cores(j, yl * 4 + z)

    def rows(j):
        if j < NCH:
            return grad_ref.at[N * j : N * (j + 1)]
        return work.at[N * (j - NCH) : N * (j - NCH + 1)]

    def scatter_y(j):
        msgs.arrive(("z", j), zrecv.at[j], d_z[0])

        def total(yl):
            parts = [zrecv[j, k, yl].astype(F32) for k in range(3)]
            return (parts[0] + parts[1]) + (parts[2] + zown[j, yl])

        ysend[j] = total(1 - y_lo).astype(BF16)
        msgs.make(("ys", j), ysend.at[j], yrecv.at[j], d_ylo)
        rows(j)[...] = total(y_lo)

    def finish(j):
        msgs.arrive(("ys", j), yrecv.at[j], d_ylo)
        rows(j)[...] = rows(j)[...] + yrecv[j].astype(F32)

    def scatter_y_first(j):
        for k in range(4):
            qsend[k] = both_cores(j, (1 - y_lo) * 4 + k).astype(BF16)
        msgs.make(("qy", j), qsend, qrecv, d_ylo)
        for k in range(4):
            qown[k] = both_cores(j, y_lo * 4 + k)

    def scatter_z_last(j):
        msgs.arrive(("qy", j), qrecv, d_ylo)
        for k in (2, 1, 3):
            at = (z + k) % 4
            zsend[j, k - 1, 0] = (qown[at] + qrecv[at].astype(F32)).astype(BF16)
            msgs.make(("z", j), zsend.at[j, k - 1, 0], zrecv.at[j, k - 1, 0], d_z[k - 1])
        rows(j)[...] = qown[z] + qrecv[z].astype(F32)

    def finish_z(j):
        msgs.arrive(("z", j), zrecv.at[j, :, 0], d_z[0])
        parts = [zrecv[j, k, 0].astype(F32) for k in range(3)]
        rows(j)[...] = (rows(j)[...] + parts[0]) + (parts[1] + parts[2])

    PARTS = {"near": (0, 6), "far": (6, 2)}
    mine = col // 2

    def multiply_part(part):
        first_rel, count = PARTS[part]
        if part == "near":
            s = place_in_stage(LAST)
        else:
            gathered(LAST)
            s = products.index(LAST) % SLOTS
        lhs = jnp.concatenate([xt[LAST, r] for r in rel[first_rel : first_rel + count]], 0)

        def tile(cols, width):
            out = jnp.dot(lhs, proj[:, cols], preferred_element_type=F32)
            out = out.reshape(count, 2, N, width)
            stage[s, 0, first_rel : first_rel + count, :, cols] = out[:, 0]
            stage[s, 1, first_rel : first_rel + count, :, cols] = out[:, 1]

        over_tiles(tile)

    def exchange_part(part):
        s = may_exchange(LAST)
        at = pl.ds(*PARTS[part])
        i = msgs.make((part, "ex"), stage.at[s, 1 - core, at], xrecv.at[s, at], d_sib)
        exchanged.setdefault(LAST, []).append(i)

    def direct(k):
        r = rel[k]
        return pltpu.make_async_remote_copy(
            src_ref=dsend.at[k],
            dst_ref=drecv.at[mine],
            send_sem=dsend_sems.at[k],
            recv_sem=drecv_sems.at[mine],
            device_id=(row, (r // 4) * 8 + (r % 4) * 2 + core),
            device_id_type=MESH,
        )

    def scatter_part(part):
        first_rel, count = PARTS[part]
        msgs.arrive((part, "ex"), xrecv.at[0, pl.ds(0, count)], d_sib)
        if (part, "ex") in msgs.arrived and len(exchanged[LAST]) == 2:
            added.add(LAST)
        for k in range(first_rel, first_rel + count):
            total = both_cores(LAST, k)
            dsend[k] = total.astype(BF16)

            @pl.when(rel[k] == mine)
            def _():
                rows(LAST)[...] = total

            @pl.when(rel[k] != mine)
            def _():
                direct(k).start()

    def finish_last():
        for k in range(1, 8):
            sender = (mine + k) % 8
            pltpu.make_async_remote_copy(
                src_ref=dsend.at[0],
                dst_ref=drecv.at[sender],
                send_sem=dsend_sems.at[0],
                recv_sem=drecv_sems.at[sender],
                device_id=d_ylo,
                device_id_type=MESH,
            ).wait_recv()
        parts = [drecv[(mine + k) % 8].astype(F32) for k in range(1, 8)]
        total = (parts[0] + parts[1]) + (parts[2] + parts[3]) + (parts[4] + parts[5])
        rows(LAST)[...] = rows(LAST)[...] + (total + parts[6])

    channel = row * CH + lax.broadcasted_iota(jnp.int32, (1, CH), 1)
    convolved = (channel >= ZW) & (channel < ZW + XW)

    def tap(k):
        return jnp.where(convolved, taps_ref[k : k + 1, :], F32(1.0 if k == 0 else 0.0))

    def number_columns():
        for q in range(TOK // 128):
            line = jnp.broadcast_to(ids_ref[q : q + 1, :].astype(F32), (128, 128))
            ids_col[128 * q : 128 * (q + 1), :] = jnp.transpose(line)

    def number_after():
        line = jnp.where(col == 15, F32(-1.0), ids_after[0:1, :].astype(F32))
        ids_col[TOK : TOK + HALO, :] = jnp.transpose(jnp.broadcast_to(line, (128, 128)))[:HALO]

    def convolve(part):
        count = 64
        if part == 0:
            for c in later_loads:
                c.start()
            for c in early_loads:
                c.wait()
            number_columns()
        taps = [tap(k) for k in range(4)]

        def step(i, _):
            t = pl.multiple_of(i * count, count)
            ids = ids_col[pl.ds(t, count + HALO), :]
            same = [ids[k : k + count] == ids[:count] for k in range(1, 4)]
            for b in range(CH // 128):
                lanes = slice(128 * b, 128 * (b + 1))
                g = cg[pl.ds(t, count + HALO), lanes].astype(F32)
                total = taps[0][:, lanes] * g[:count]
                for k in range(1, 4):
                    term = taps[k][:, lanes] * g[k : k + count]
                    total = total + jnp.where(same[k - 1], term, F32(0.0))
                proj[pl.ds(t, count), lanes] = total.astype(BF16)
            return 0

        if part == 3:
            msgs.arrive("halo", cg.at[pl.ds(TOK, HALO)], d_prev)
            msgs.arrive("ids", ids_after, d_prev)
            number_after()
        lax.fori_loop(8 * part, 8 * part + 8, step, 0)
        if part == 3:
            for c in later_loads:
                c.wait()
            for t in range(STRIPS):
                high, low = split(right_basis[:, strip(t)])
                cg[strip(t), :RB] = high
                cg[strip(t), 512 : 512 + RB] = low

    def strip(t):
        return slice(RB * t, RB * (t + 1))

    def q_right(t):
        return cg[strip(t), :RB], cg[strip(t), 512 : 512 + RB]

    msgs.make("halo", cg_hbm.at[pl.ds(0, HALO)], cg.at[pl.ds(TOK, HALO)], d_prev)
    msgs.make("ids", ids_hbm.at[pl.ds(0, 8)], ids_after, d_prev)
    steps = {
        "xo": send_own,
        "fo": forward_own,
        "y": send_y,
        "xq": send_across,
        "fq": forward_across,
        "ys": send_y_sides,
        "yf": send_y_far,
        "conv": convolve,
        "mul": multiply,
        "ex": exchange,
        "sz": scatter_z,
        "sy": scatter_y,
        "fin": finish,
        "mulp": multiply_part,
        "exp": exchange_part,
        "scp": scatter_part,
    }
    for name, j in ORDER:
        steps[name](j)
    finish_last()

    place = lax.broadcasted_iota(jnp.int32, (RB, 16 * 32), 1)
    source = lax.broadcasted_iota(jnp.int32, (RB, 16 * 32), 0)
    chosen = (place % 32 < RSHARE) & (place // 32 * RSHARE + place % 32 == source)
    one_hot = jnp.where(chosen, F32(1.0), F32(0.0)).astype(BF16)
    slots = [place_in_stage(j) for j in GRAMS]
    for t in range(STRIPS):
        band = grad_ref[:, strip(t)].astype(BF16)
        placed = jnp.dot(band, one_hot, preferred_element_type=F32).astype(BF16)
        block = contract(placed, band, 0, 0).reshape(8, 2, 2, N, RB)
        for h, s in enumerate(slots):
            even, odd = block[:, 0, h], block[:, 1, h]
            stage[s, 0, :, :, strip(t)] = jnp.where(core == 0, even, odd)
            gsend[h, :, :, strip(t)] = jnp.where(core == 0, odd, even).astype(BF16)
    for h in range(2):
        msgs.make(("gram", h), gsend.at[h], grecv.at[h], d_sib)

    rounded = grad_ref[...].astype(BF16)
    left = contract(rounded, rounded, 1, 1)
    for r in range(8):
        share = left[LSHARE * r : LSHARE * (r + 1)]
        left_send[r] = jnp.concatenate([share, jnp.zeros((32 - LSHARE, BL), F32)], 0).astype(BF16)
    for k in range(1, 8):
        msgs.make("left", left_send.at[(row + k) % 8], left_recv.at[k - 1], d_row[k - 1])

    q_left = split(left_basis[...])
    msgs.arrive(("gram", 0), grecv.at[0], d_sib)
    scatter_z(GRAMS[0])
    msgs.arrive(("gram", 1), grecv.at[1], d_sib)
    scatter_y_first(GRAMS[1])
    grad_parts = split(grad_ref[...])
    grad_ref[...] = contract3(q_left, grad_parts, 0, 0)

    def moments(t):
        rotated = contract3(split(grad_ref[:, strip(t)]), q_right(t), 1, 1)
        new_first = 0.9 * first[:, strip(t)] + 0.1 * rotated
        new_second = 0.95 * second[:, strip(t)] + 0.05 * rotated * rotated
        first[:, strip(t)] = new_first
        second[:, strip(t)] = new_second
        grad_ref[:, strip(t)] = new_first / (jnp.sqrt(new_second) + 1e-08)

    for t in range(STRIPS):
        moments(t)
    scatter_z_last(GRAMS[1])
    stores = [
        pltpu.make_async_copy(src, dst, local_sems.at[10 + i])
        for i, (src, dst) in enumerate(
            [
                (first, first_out),
                (second, second_out),
                (grad_ref, direction_out),
                (left_stat, new_left_out),
                (right_stat, new_right_out),
            ]
        )
    ]
    stores[0].start()
    stores[1].start()
    grad_ref[...] = contract3(q_left, split(grad_ref[...]), 1, 0)
    scatter_y(GRAMS[0])
    for t in range(STRIPS):
        grad_ref[:, strip(t)] = contract3(split(grad_ref[:, strip(t)]), q_right(t), 1, 0)
    stores[2].start()

    msgs.arrive("left", left_recv, d_row[0])
    total = left_send[row].astype(F32)
    for k in range(7):
        total = total + left_recv[k].astype(F32)
    left_stat[...] = 0.9 * left_stat[...] + 0.1 * (total[:LSHARE] / OUTPUT_CHANNELS)
    stores[3].start()

    finish_z(GRAMS[1])
    finish(GRAMS[0])
    right_stat[...] = 0.9 * right_stat[...] + 0.1 * (work[:RSHARE, :] / MODEL_WIDTH)
    stores[4].start()
    for i in range(len(msgs.copies)):
        msgs.release(i)
    for k in range(8):

        @pl.when(rel[k] != mine)
        def _():
            direct(k).wait_send()

    for c in stores:
        c.wait()


PIECES = 4


def copy_kernel(*refs):
    count = (len(refs) - 2) // 3
    in_sems, out_sems = refs[-2:]
    loads, stores = [], []
    for src, dst, held in zip(refs[:count], refs[count : 2 * count], refs[2 * count : -2]):
        pieces = PIECES if src.shape[0] == BL else 1
        height = src.shape[0] // pieces
        for i in range(pieces):
            at = pl.ds(i * height, height)
            k = len(loads)
            loads.append(pltpu.make_async_copy(src.at[at], held.at[at], in_sems.at[k]))
            stores.append(pltpu.make_async_copy(held.at[at], dst.at[at], out_sems.at[k]))
    for c in loads:
        c.start()
    for c, d in zip(loads, stores):
        c.wait()
        d.start()
    for d in stores:
        d.wait()


def shards(
    layer_input,
    conv_grad,
    conv_kernel,
    segment_ids,
    left_basis,
    right_basis,
    left_stat,
    right_stat,
    first_moment,
    second_moment,
):
    any_spec = pl.BlockSpec(memory_space=pl.ANY)
    block = jax.ShapeDtypeStruct((BL, CH), F32)
    out_shape = [
        block,
        block,
        block,
        jax.ShapeDtypeStruct((LSHARE, BL), F32),
        jax.ShapeDtypeStruct((RSHARE, CH), F32),
    ]
    results = pl.pallas_call(
        step_kernel,
        out_shape=out_shape,
        in_specs=[any_spec] * 10,
        out_specs=[any_spec] * 5,
        scratch_shapes=[
            pltpu.VMEM((TOK, FEAT), BF16),
            pltpu.VMEM((TOK + HALO, CH), BF16),
            pltpu.VMEM((4, CH), F32),
            pltpu.VMEM((TOK // 128, 128), jnp.int32),
            pltpu.VMEM((TOK, CH), BF16),
            pltpu.VMEM((TOK + HALO, 128), F32),
            pltpu.VMEM((8, 128), jnp.int32),
            pltpu.VMEM((NCH, 8, 2 * N, TOK), BF16),
            pltpu.VMEM((SLOTS, 2, 8, N, CH), F32),
            pltpu.VMEM((SLOTS, 8, N, CH), F32),
            pltpu.VMEM((NALL, 3, 2, N, CH), BF16),
            pltpu.VMEM((NALL, 3, 2, N, CH), BF16),
            pltpu.VMEM((NALL, 2, N, CH), F32),
            pltpu.VMEM((NALL, N, CH), BF16),
            pltpu.VMEM((NALL, N, CH), BF16),
            pltpu.VMEM((4, N, CH), BF16),
            pltpu.VMEM((4, N, CH), BF16),
            pltpu.VMEM((4, N, CH), F32),
            pltpu.VMEM((2, 8, N, CH), BF16),
            pltpu.VMEM((2, 8, N, CH), BF16),
            pltpu.VMEM((8, N, CH), BF16),
            pltpu.VMEM((8, N, CH), BF16),
            pltpu.VMEM((BL, CH), F32),
            pltpu.VMEM((BL, CH), F32),
            pltpu.VMEM((BL, CH), F32),
            pltpu.VMEM((2 * N, CH), F32),
            pltpu.VMEM((RB, CH), F32),
            pltpu.VMEM((RSHARE, CH), F32),
            pltpu.VMEM((BL, BL), F32),
            pltpu.VMEM((LSHARE, BL), F32),
            pltpu.VMEM((8, 32, BL), BF16),
            pltpu.VMEM((7, 32, BL), BF16),
            pltpu.SemaphoreType.DMA((15,)),
            pltpu.SemaphoreType.DMA((POOL,)),
            pltpu.SemaphoreType.DMA((NGROUP,)),
            pltpu.SemaphoreType.DMA((8,)),
            pltpu.SemaphoreType.DMA((8,)),
        ],
        name="step",
        cost_estimate=pl.CostEstimate(
            flops=2 * MODEL_WIDTH * TOK * CH, bytes_accessed=20_000_000, transcendentals=0
        ),
        compiler_params=pltpu.CompilerParams(
            collective_id=0, has_side_effects=True, vmem_limit_bytes=63 << 20
        ),
    )(
        layer_input,
        conv_grad,
        conv_kernel,
        segment_ids.reshape(TOK // 128, 128),
        right_basis.T,
        first_moment,
        second_moment,
        right_stat.T,
        left_basis,
        left_stat.T,
    )
    first, second, direction, new_left, new_right = pl.pallas_call(
        copy_kernel,
        out_shape=out_shape,
        in_specs=[any_spec] * 5,
        out_specs=[any_spec] * 5,
        scratch_shapes=[
            *[pltpu.VMEM(a.shape, F32) for a in out_shape],
            pltpu.SemaphoreType.DMA((3 * PIECES + 2,)),
            pltpu.SemaphoreType.DMA((3 * PIECES + 2,)),
        ],
        name="hand_over",
    )(*results)
    return new_left.T, new_right.T, first, second, direction


def solution(mesh):
    placed = (
        P("col", "row"),
        P("col", "row"),
        P(None, "row"),
        P("col"),
        P("col", None),
        P("row", None),
        P("col", "row"),
        P("row", "col"),
        P("col", "row"),
        P("col", "row"),
    )
    return jax.shard_map(
        shards,
        mesh=mesh,
        in_specs=placed,
        out_specs=(
            P("col", "row"),
            P("row", "col"),
            P("col", "row"),
            P("col", "row"),
            P("col", "row"),
        ),
        check_vma=False,
    )
```
